32 devices in a mesh: groups: 2 (over y), seq: 4 (over z), head: 2 (over x), section: 2 (over core).
Axes of the slice: x: 2, y: 2, z: 4, core: 2. Of those that a mesh axis runs over, the one named last changes fastest.
Arguments:
- q_heads: bfloat16 [2, 1024, 12288], P('section', ('groups', 'seq'), 'head'), parts along dimension 1, may hold values from -256 to 256
- cache_latent: bfloat16 [2, 1024, 512], P('section', ('groups', 'seq')), parts along dimension 1, may hold values from -6 to 6
- cache_rope: bfloat16 [2, 1024, 64], P('section', ('groups', 'seq')), parts along dimension 1, may hold values from -6.5 to 6.5
- span_start: int32 [2, 4], P('section', 'groups'), parts along dimension 1, may hold values from 1 to 256, as said below
- prefix_len: int32 [2, 4], P('section', 'groups'), parts along dimension 1, may hold values from 0 to 256, as said below
- key_up: bfloat16 [2, 64, 128, 512], P('section', 'head'), may hold values from -0.5 to 0.5
- value_up: bfloat16 [2, 64, 512, 128], P('section', 'head'), may hold values from -2 to 2
- out_weight: bfloat16 [2, 8192, 7168], P('section', 'head', 'seq'), may hold values from -0.0625 to 0.0625
Outputs:
- mixed_out: bfloat16 [2, 1024, 7168], P('section', ('groups', 'head'), 'seq'), parts along dimension 1
The draws below stay inside these ranges and needn't reach their ends.
There are 2 independent parts, one for each index of `groups`. The reference program is written for one: setup_inputs(seed, part) draws one part's arguments, and reference() takes and returns one part's arrays. A program takes and returns all parts, laid end to end along the dimension named above; an argument that names none is the same for every part. Nothing has to cross between parts.
Inputs may be any that keep to these rules, and one draw needn't show every extreme that they name: Span j's own tokens are context positions span_start to span_start + 255; the last span of every layer starts at 256. `prefix_len`: below the span's span_start for every span but the last; equal to it for the last span of every layer.
All inputs are finite; a program needn't handle non-finite values.
Results may differ from the reference program's by a relative error of at most 0.0085.
Values may be sent and summed in bfloat16 or wider, within the bound.
A program may use at most 64 MiB of HBM per device.

```python
import jax
import jax.numpy as jnp
from jax import lax

D = 7168
HEADS = 64
NOPE = 128
ROPE = 64
LAT = 512
VDIM = 128
NSPAN = 2
LAYERS = 2
QT = 512
CTX = 512
SPAN = 256


def span_layout(key):
    first_key, second_key = jax.random.split(jax.random.fold_in(key, 11))
    last_start = CTX - SPAN
    grid_shape = (LAYERS, NSPAN)
    is_last = jnp.arange(NSPAN)[None, :] == NSPAN - 1
    drawn_first = jax.random.randint(first_key, grid_shape, 1, last_start + 1)
    span_first = jnp.where(is_last, last_start, drawn_first)
    drawn_prefix = jax.random.randint(second_key, grid_shape, 0, jnp.maximum(span_first, 1))
    prefix_row = jnp.where(is_last, span_first, drawn_prefix)
    return (span_first.astype(jnp.int32), prefix_row.astype(jnp.int32))


def draw_span_start(key, part):
    return span_layout(key)[0]


def draw_prefix_len(key, part):
    return span_layout(key)[1]


def draw_cache_rope(key, part):
    drawn = jnp.clip(jax.random.normal(jax.random.fold_in(key, 21), (LAYERS, CTX, ROPE), jnp.float32), -6.0, 6.0)
    return drawn.astype(jnp.bfloat16)


def draw_q_heads(key, part):
    width_all = NOPE + ROPE
    drawn = jnp.clip(jax.random.normal(jax.random.fold_in(key, 31), (LAYERS, QT, HEADS, width_all), jnp.float32), -6.0, 6.0)
    return drawn.reshape(LAYERS, QT, HEADS * width_all).astype(jnp.bfloat16)


def steps_of(key, extent, cuts, smallest, top_value):
    factor_of = 1.0
    for position, blocks in cuts:
        draws = jax.random.uniform(jax.random.fold_in(jax.random.fold_in(key, 6), position), (blocks,), jnp.float32, smallest / len(cuts), top_value / len(cuts))
        factor_of = factor_of * jnp.repeat(jnp.exp(draws), extent[position] // blocks).reshape((-1,) + (1,) * (len(extent) - 1 - position))
    return factor_of


def normal_values(key, shape, deviation, reach, shards=(), kind=jnp.bfloat16):
    array = deviation * jax.random.normal(key, shape, jnp.float32)
    if shards:
        array = array * steps_of(key, shape, shards, -0.22, 0.18)
    return jnp.clip(array, -reach, reach).astype(kind)


def setup_inputs(seed: int = 0, part: int = 0) -> dict:
    arg_keys = jax.random.split(jax.random.key(seed), 9)
    part_keys = jax.random.split(jax.random.fold_in(arg_keys[8], part), 9)
    q_heads = draw_q_heads(jax.random.fold_in(jax.random.fold_in(arg_keys[8], part), 71), part)
    cache_latent = normal_values(part_keys[1], (LAYERS, CTX, LAT), 1.0, 6.0, ((0, 2), (1, 4)))
    cache_rope = draw_cache_rope(jax.random.fold_in(jax.random.fold_in(arg_keys[8], part), 71), part)
    span_start = draw_span_start(jax.random.fold_in(jax.random.fold_in(arg_keys[8], part), 71), part)
    prefix_len = draw_prefix_len(jax.random.fold_in(jax.random.fold_in(arg_keys[8], part), 71), part)
    key_up = normal_values(arg_keys[5], (LAYERS, HEADS, NOPE, LAT), NOPE ** -0.5, 0.5, ((0, 2), (1, 2)))
    value_up = normal_values(arg_keys[6], (LAYERS, HEADS, LAT, VDIM), 0.15, 2.0, ((0, 2), (1, 2)))
    out_weight = normal_values(arg_keys[7], (LAYERS, HEADS * VDIM, D), (HEADS * VDIM) ** -0.5, 0.0625, ((0, 2), (1, 2), (2, 4)))
    return {"q_heads": q_heads, "cache_latent": cache_latent, "cache_rope": cache_rope, "span_start": span_start, "prefix_len": prefix_len, "key_up": key_up, "value_up": value_up, "out_weight": out_weight}


def reference(q_heads, cache_latent, cache_rope, span_start, prefix_len, key_up, value_up, out_weight):
    softmax_scale = (NOPE + ROPE) ** -0.5
    token_ids = jnp.arange(QT, dtype=jnp.int32)
    span_ids = token_ids // SPAN
    in_span = token_ids % SPAN
    key_pos = jnp.arange(CTX, dtype=jnp.int32)
    results = []
    for layer_idx in range(LAYERS):
        span_first = span_start[layer_idx][span_ids]
        prefix_row = prefix_len[layer_idx][span_ids]
        positions = span_first + in_span
        visible = (key_pos[None, :] < prefix_row[:, None]) | ((key_pos[None, :] >= span_first[:, None]) & (key_pos[None, :] <= positions[:, None]))
        queries = q_heads[layer_idx].reshape(QT, HEADS, NOPE + ROPE)
        latent = cache_latent[layer_idx]
        rope_keys = cache_rope[layer_idx]

        def one_head(inputs):
            query_head, key_map, value_map = inputs
            absorbed = jnp.dot(query_head[:, :NOPE], key_map, preferred_element_type=jnp.float32).astype(jnp.bfloat16)
            scores = (jnp.dot(absorbed, latent.T, preferred_element_type=jnp.float32) + jnp.dot(query_head[:, NOPE:], rope_keys.T, preferred_element_type=jnp.float32)) * softmax_scale
            scores = jnp.where(visible, scores, -jnp.inf)
            peak_score = jnp.max(scores, axis=1, keepdims=True)
            weights = jnp.where(visible, jnp.exp(scores - peak_score), 0.0)
            row_total = jnp.sum(weights, axis=1, keepdims=True)
            rounded = weights.astype(jnp.bfloat16)
            latent_out = (jnp.dot(rounded, latent, preferred_element_type=jnp.float32) / row_total).astype(jnp.bfloat16)
            return jnp.dot(latent_out, value_map, preferred_element_type=jnp.float32).astype(jnp.bfloat16)

        head_outs = lax.map(one_head, (jnp.swapaxes(queries, 0, 1), key_up[layer_idx], value_up[layer_idx]))
        joined = jnp.swapaxes(head_outs, 0, 1).reshape(QT, HEADS * VDIM)
        results.append(jnp.dot(joined, out_weight[layer_idx], preferred_element_type=jnp.float32).astype(jnp.bfloat16))
    return jnp.stack(results)
```

```python
import jax
import jax.numpy as jnp
from jax import lax
from jax.sharding import PartitionSpec as P

NSPAN = 2

masked_fill = -1e30


def on_device(
    q_heads, cache_latent, cache_rope, span_start, prefix_len, key_up, value_up, out_weight
):
    f32, bf16 = jnp.float32, jnp.bfloat16
    queries_flat = q_heads[0]
    tokens = queries_flat.shape[0]
    head_count, nope_dim, lat_dim = key_up.shape[1:]
    value_dim = value_up.shape[3]
    head_width = queries_flat.shape[1] // head_count
    seq_count = lax.axis_size("seq")
    seq_index = lax.axis_index("seq")
    x_count = lax.axis_size("head")
    x_index = lax.axis_index("head")
    softmax_scale = head_width ** (-0.5)
    span_len = tokens * seq_count // NSPAN

    keys = lax.all_gather(
        jnp.concatenate([cache_latent[0], cache_rope[0]], axis=1), "seq", axis=0, tiled=True
    )
    latents = keys[:, :lat_dim]

    queries = queries_flat.reshape(tokens, head_count, head_width)
    absorbed = jnp.einsum(
        "thn,hnl->htl", queries[:, :, :nope_dim], key_up[0], preferred_element_type=f32
    ).astype(bf16)
    rope_query = jnp.swapaxes(queries[:, :, nope_dim:], 0, 1)
    wide = jnp.concatenate([absorbed, rope_query], axis=2)

    global_row = seq_index * tokens + jnp.arange(tokens, dtype=jnp.int32)
    one_hot = (global_row // span_len)[:, None] == jnp.arange(NSPAN, dtype=jnp.int32)[None, :]
    span_first = jnp.sum(jnp.where(one_hot, span_start[0][None, :], 0), axis=1)
    prefix_row = jnp.sum(jnp.where(one_hot, prefix_len[0][None, :], 0), axis=1)
    token_pos = span_first + global_row % span_len
    key_pos = jnp.arange(keys.shape[0], dtype=jnp.int32)
    visible = (
        (key_pos[None, :] < prefix_row[:, None])
        | (key_pos[None, :] >= span_first[:, None]) & (key_pos[None, :] <= token_pos[:, None])
    )[None]

    chunks = 4
    per = head_count // chunks
    gathered = []
    for c in range(chunks):
        sl = slice(c * per, (c + 1) * per)
        scores = jnp.einsum("htl,kl->htk", wide[sl], keys, preferred_element_type=f32)
        scores = jnp.where(visible, scores * softmax_scale, masked_fill)
        peak = jnp.max(scores, axis=2, keepdims=True)
        weights = jnp.exp(scores - peak)
        totals = jnp.sum(weights, axis=2, keepdims=True)
        summed = jnp.einsum("htk,kl->htl", weights.astype(bf16), latents, preferred_element_type=f32)
        latent_out = (summed / totals).astype(bf16)
        head_out = jnp.einsum("htl,hlv->htv", latent_out, value_up[0, sl], preferred_element_type=f32)
        head_out = jnp.swapaxes(head_out.astype(bf16), 0, 1).reshape(tokens, per * value_dim)
        gathered.append(lax.all_gather(head_out, "seq", axis=0, tiled=True))

    weight = out_weight[0]
    cut = per * value_dim * (chunks - 1)
    early = jnp.dot(
        jnp.concatenate(gathered[:-1], axis=1), weight[:cut], preferred_element_type=f32
    )
    rows = early.shape[0] // x_count

    def piece(target):
        late = lax.dynamic_slice_in_dim(gathered[-1], target * rows, rows, 0)
        return lax.dynamic_slice_in_dim(early, target * rows, rows, 0) + jnp.dot(
            late, weight[cut:], preferred_element_type=f32
        )

    arrived = []
    for shift in range(1, x_count):
        part = piece((x_index + shift) % x_count).astype(bf16)
        perm = [(i, (i + shift) % x_count) for i in range(x_count)]
        arrived.append(lax.ppermute(part, "head", perm))
    total = piece(x_index)
    for part in arrived:
        total = total + part.astype(f32)
    return total.astype(bf16)[None]


def solution(mesh):
    in_specs = (
        P("section", ("groups", "seq"), "head"),
        P("section", ("groups", "seq"), None),
        P("section", ("groups", "seq"), None),
        P("section", "groups"),
        P("section", "groups"),
        P("section", "head", None, None),
        P("section", "head", None, None),
        P("section", "head", "seq"),
    )
    out_specs = P("section", ("groups", "head"), "seq")
    return jax.shard_map(
        on_device, mesh=mesh, in_specs=in_specs, out_specs=out_specs, check_vma=False
    )
```

```python
import functools
import math

import jax
import jax.numpy as jnp
from jax import lax
from jax.experimental import pallas as pl
from jax.experimental.pallas import tpu as pltpu
from jax.sharding import PartitionSpec as P

NSPAN = 2
SPLIT = 2
masked_fill = -1e30
f32, bf16 = jnp.float32, jnp.bfloat16


def kernel(
    n, xn, kv_ref, start_ref, prefix_ref, q_hbm, ku_hbm, vu_hbm, w_hbm, out_ref,
    keys, q, ku, vu, w, wide, bias, full, acc, xs, xr,
    lsem, kv_ssem, kv_rsem, z_ssem, z_rsem, x_ssem, x_rsem,
):
    me = lax.axis_index("seq")
    xi = lax.axis_index("head")
    tokens = kv_ref.shape[0]
    heads, nope, lat = ku.shape
    vdim = vu.shape[2]
    pair = 2 * q.shape[1] // heads
    rope = pair // 2 - nope
    units, hgs, ts, hw = full.shape
    hg_heads = hw // vdim
    upx, ntiles, _, nt = acc.shape
    ctx = n * tokens
    scale = math.log2(math.e) * (pair // 2) ** (-0.5)

    loads = [
        pltpu.make_async_copy(a, b, lsem.at[i])
        for i, (a, b) in enumerate(((q_hbm, q), (ku_hbm, ku), (vu_hbm, vu), (w_hbm, w)))
    ]
    for load in loads:
        load.start()

    barrier = pltpu.get_barrier_semaphore()
    has_left, has_right = me > 0, me < n - 1

    def greet(**where):
        pl.semaphore_signal(
            barrier, inc=1, device_id=where, device_id_type=pl.DeviceIdType.MESH
        )

    @pl.when(has_left)
    def _():
        greet(seq=me - 1)

    @pl.when(has_right)
    def _():
        greet(seq=me + 1)

    for s in range(1, xn):
        greet(head=lax.rem(xi + s, xn))

    for part in range(SPLIT):
        keys[me * SPLIT + part] = kv_ref[part * ts : (part + 1) * ts, :]

    met = xn - 1 + jnp.minimum(me, 1) + jnp.minimum(n - 1 - me, 1)
    pl.semaphore_wait(barrier, met)

    def kv_copy(i, way):
        return pltpu.make_async_remote_copy(
            src_ref=keys.at[i],
            dst_ref=keys.at[i],
            send_sem=kv_ssem.at[way, i],
            recv_sem=kv_rsem.at[i],
            device_id={"seq": me - 1 + 2 * way},
            device_id_type=pl.DeviceIdType.MESH,
        )

    def z_copy(unit, hg, way):
        return pltpu.make_async_remote_copy(
            src_ref=full.at[unit, hg],
            dst_ref=full.at[unit, hg],
            send_sem=z_ssem.at[way, unit, hg],
            recv_sem=z_rsem.at[unit, hg],
            device_id={"seq": me - 1 + 2 * way},
            device_id_type=pl.DeviceIdType.MESH,
        )

    def send_own(make):
        @pl.when(has_left)
        def _():
            make(0).start()

        @pl.when(has_right)
        def _():
            make(1).start()

    def take(make, d, wait=True):
        @pl.when(me + d < n)
        def _():
            make(me + d, 1).wait_recv()

            @pl.when(has_left)
            def _():
                make(me + d, 0).start()

        @pl.when(me - d >= 0)
        def _():
            make(me - d, 0).wait_recv()

            @pl.when(has_right)
            def _():
                make(me - d, 1).start()

    for part in range(SPLIT):
        send_own(lambda way, part=part: kv_copy(me * SPLIT + part, way))

    def absorb(i, _):
        block = q[:, pl.ds(pl.multiple_of(i * pair, pair), pair)]
        lead = jnp.zeros((rope, lat), bf16)
        tail = lead
        first = jnp.dot(block[:, :nope], ku[2 * i], preferred_element_type=f32)
        second = jnp.dot(
            block[:, nope:],
            jnp.concatenate([lead, ku[2 * i + 1], tail], axis=0),
            preferred_element_type=f32,
        )
        lane = lax.broadcasted_iota(jnp.int32, (tokens, 2 * rope), 1)
        zero = jnp.zeros((tokens, 2 * rope), bf16)
        wide[2 * i, :, :lat] = first.astype(bf16)
        wide[2 * i + 1, :, :lat] = second.astype(bf16)
        wide[2 * i, :, lat:] = jnp.where(lane < rope, block[:, nope : nope + 2 * rope], zero)
        wide[2 * i + 1, :, lat:] = jnp.where(lane >= rope, block[:, pair - 2 * rope :], zero)
        return 0

    loads[0].wait()
    loads[1].wait()

    span_len = ctx // NSPAN
    span = me * tokens // span_len
    first_pos = start_ref[0, span]
    prefix = prefix_ref[0, span]
    row_pos = first_pos + me * tokens % span_len + lax.broadcasted_iota(jnp.int32, (tokens, ctx), 0)
    key_pos = lax.broadcasted_iota(jnp.int32, (tokens, ctx), 1)
    visible = (key_pos < prefix) | ((key_pos >= first_pos) & (key_pos <= row_pos))
    bias[...] = jnp.where(visible, 0.0, masked_fill)

    half = heads // 4
    lax.fori_loop(0, half, absorb, 0)
    for d in range(1, n):
        for part in range(SPLIT):
            take(lambda src, way, part=part: kv_copy(src * SPLIT + part, way), d)
        if d == 1:
            lax.fori_loop(half, heads // 2, absorb, 0)
    loads[2].wait()

    def attend(m, _):
        tb, hg = m // hgs, lax.rem(m, hgs)
        rows = pl.ds(pl.multiple_of(tb * ts, ts), ts)
        unit = me * SPLIT + tb
        all_keys = keys[...].reshape(ctx, keys.shape[2])
        hide = bias[rows, :]
        for p in range(hg_heads // 2):
            h = hg * hg_heads + 2 * p
            wq = wide[pl.ds(h, 2), rows, :].reshape(2 * ts, wide.shape[2])
            scores = lax.dot_general(
                wq, all_keys, (((1,), (1,)), ((), ())), preferred_element_type=f32
            )
            scores = scores * scale + jnp.concatenate([hide, hide], axis=0)
            peak = jnp.max(scores, axis=1, keepdims=True)
            weights = jnp.exp2(scores - peak)
            total = jnp.sum(weights, axis=1, keepdims=True)
            mixed = jnp.dot(weights.astype(bf16), all_keys[:, :lat], preferred_element_type=f32)
            mixed = (mixed / total).astype(bf16)
            for k in range(2):
                value = jnp.dot(
                    mixed[k * ts : (k + 1) * ts], vu[h + k], preferred_element_type=f32
                )
                lo = (2 * p + k) * vdim
                full[unit, hg, :, lo : lo + vdim] = value.astype(bf16)
        send_own(lambda way: z_copy(unit, hg, way))
        return 0

    lax.fori_loop(0, SPLIT * hgs, attend, 0)

    def x_copy(unit, t):
        return pltpu.make_async_remote_copy(
            src_ref=xs.at[unit, t],
            dst_ref=xr.at[xi, lax.rem(unit, upx), t],
            send_sem=x_ssem.at[unit, t],
            recv_sem=x_rsem.at[xi, lax.rem(unit, upx), t],
            device_id={"head": unit // upx},
            device_id_type=pl.DeviceIdType.MESH,
        )

    def project(unit):
        mine = unit // upx == xi

        def tile(t, _):
            total = jnp.zeros((ts, nt), f32)
            for hg in range(hgs):
                if ntiles == 1:
                    part = w[hg * hw : (hg + 1) * hw, :]
                else:
                    part = w[hg * hw : (hg + 1) * hw, pl.ds(pl.multiple_of(t * nt, nt), nt)]
                total += jnp.dot(full[unit, hg], part, preferred_element_type=f32)

            @pl.when(mine)
            def _():
                acc[lax.rem(unit, upx), t] = total

            @pl.when(jnp.logical_not(mine))
            def _():
                xs[unit, t] = total.astype(bf16)
                x_copy(unit, t).start()

            return 0

        lax.fori_loop(0, ntiles, tile, 0)

    loads[3].wait()

    for tb in range(SPLIT):
        project(me * SPLIT + tb)

    def gather(i, _):
        d, tb = 1 + i // SPLIT, lax.rem(i, SPLIT)
        for hg in range(hgs):
            take(lambda src, way, hg=hg: z_copy(src * SPLIT + tb, hg, way), d)

        @pl.when(me + d < n)
        def _():
            project((me + d) * SPLIT + tb)

        @pl.when(me - d >= 0)
        def _():
            project((me - d) * SPLIT + tb)

        return 0

    lax.fori_loop(0, (n - 1) * SPLIT, gather, 0)

    def sent(i, _):
        unit = i
        left = has_left & (unit >= me * SPLIT)
        right = has_right & (unit < (me + 1) * SPLIT)
        for way, did in ((0, left), (1, right)):

            @pl.when(did)
            def _():
                kv_copy(unit, way).wait_send()
                for hg in range(hgs):
                    z_copy(unit, hg, way).wait_send()

        return 0

    lax.fori_loop(0, units, sent, 0)

    for lu in range(upx):
        for t in range(ntiles):
            total = acc[lu, t]
            for s in range(1, xn):
                peer = lax.rem(xi + s, xn)
                pltpu.make_async_remote_copy(
                    src_ref=xs.at[0, t],
                    dst_ref=xr.at[peer, lu, t],
                    send_sem=x_ssem.at[0, t],
                    recv_sem=x_rsem.at[peer, lu, t],
                    device_id={"head": peer},
                    device_id_type=pl.DeviceIdType.MESH,
                ).wait_recv()
                total = total + xr[peer, lu, t].astype(f32)
            out_ref[lu * ts : (lu + 1) * ts, t * nt : (t + 1) * nt] = total.astype(bf16)

    def x_sent(i, _):
        @pl.when(i // upx != xi)
        def _():
            for t in range(ntiles):
                x_copy(i, t).wait_send()

        return 0

    lax.fori_loop(0, units, x_sent, 0)


def on_device(
    n, xn, q_heads, cache_latent, cache_rope, span_start, prefix_len, key_up, value_up, out_weight
):
    heads, nope, lat = key_up.shape[1:]
    vdim = value_up.shape[3]
    tokens = q_heads.shape[1]
    rope = cache_rope.shape[2]
    rows_all, width = out_weight.shape[1:]
    keys = jnp.concatenate([cache_latent[0], cache_rope[0], cache_rope[0]], axis=1)
    kw = lat + 2 * rope
    ts = tokens // SPLIT
    units = n * SPLIT
    upx = units // xn
    hg_heads = math.gcd(8, heads)
    hgs = heads // hg_heads
    nt = 256 if width % 256 == 0 else width
    ntiles = width // nt
    ctx = n * tokens
    vmem, smem = pltpu.VMEM, pltpu.SMEM
    hbm = pl.BlockSpec(memory_space=pl.ANY)
    out = pl.pallas_call(
        functools.partial(kernel, n, xn),
        out_shape=jax.ShapeDtypeStruct((upx * ts, width), bf16),
        in_specs=[
            pl.BlockSpec(memory_space=vmem),
            pl.BlockSpec(memory_space=smem),
            pl.BlockSpec(memory_space=smem),
            hbm,
            hbm,
            hbm,
            hbm,
        ],
        out_specs=pl.BlockSpec(memory_space=vmem),
        scratch_shapes=[
            vmem((units, ts, kw), bf16),
            vmem(q_heads.shape[1:], bf16),
            vmem(key_up.shape[1:], bf16),
            vmem(value_up.shape[1:], bf16),
            vmem((rows_all, width), bf16),
            vmem((heads, tokens, kw), bf16),
            vmem((tokens, ctx), f32),
            vmem((units, hgs, ts, hg_heads * vdim), bf16),
            vmem((upx, ntiles, ts, nt), f32),
            vmem((units, ntiles, ts, nt), bf16),
            vmem((xn, upx, ntiles, ts, nt), bf16),
            pltpu.SemaphoreType.DMA((4,)),
            pltpu.SemaphoreType.DMA((2, units)),
            pltpu.SemaphoreType.DMA((units,)),
            pltpu.SemaphoreType.DMA((2, units, hgs)),
            pltpu.SemaphoreType.DMA((units, hgs)),
            pltpu.SemaphoreType.DMA((units, ntiles)),
            pltpu.SemaphoreType.DMA((xn, upx, ntiles)),
        ],
        compiler_params=pltpu.CompilerParams(
            collective_id=0, has_side_effects=True, vmem_limit_bytes=56 * 1024 * 1024
        ),
        cost_estimate=pl.CostEstimate(
            flops=2 * ctx * rows_all * width + 4 * tokens * heads * ctx * kw,
            bytes_accessed=2 * rows_all * width,
            transcendentals=tokens * heads * ctx,
        ),
    )(keys, span_start, prefix_len, q_heads[0], key_up[0], value_up[0], out_weight[0])
    return out[None]


def solution(mesh):
    in_specs = (
        P("section", ("groups", "seq"), "head"),
        P("section", ("groups", "seq"), None),
        P("section", ("groups", "seq"), None),
        P("section", "groups"),
        P("section", "groups"),
        P("section", "head", None, None),
        P("section", "head", None, None),
        P("section", "head", "seq"),
    )
    out_specs = P("section", ("groups", "head"), "seq")
    return jax.shard_map(
        functools.partial(on_device, mesh.shape["seq"], mesh.shape["head"]),
        mesh=mesh,
        in_specs=in_specs,
        out_specs=out_specs,
        check_vma=False,
    )
```

```python
import functools
import math

import jax
import jax.numpy as jnp
from jax import lax
from jax.experimental import pallas as pl
from jax.experimental.pallas import tpu as pltpu
from jax.sharding import PartitionSpec as P

NSPAN = 2
SPLIT = 4
masked_fill = -1e30
f32, bf16 = jnp.float32, jnp.bfloat16


def kernel(
    n, xn, lat_ref, rope_ref, start_ref, prefix_ref, q_hbm, ku_hbm, vu_hbm, w_hbm, out_ref,
    keys, q, ku, vu, w, wide, bias, full, acc, xs, xr,
    lsem, kv_ssem, kv_rsem, kx_ssem, z_ssem, z_rsem, x_ssem, x_rsem,
):
    me = lax.axis_index("seq")
    xi = lax.axis_index("head")
    tokens = lat_ref.shape[0]
    heads, nope, lat = ku.shape
    vdim = vu.shape[2]
    pair = 2 * q.shape[1] // heads
    rope = pair // 2 - nope
    units, hgs, ts, hw = full.shape
    hg_heads = hw // vdim
    batch = min(4, hg_heads)
    upx, ntiles, _, nt = acc.shape
    ctx = n * tokens
    scale = math.log2(math.e) * (pair // 2) ** (-0.5)

    loads = [
        pltpu.make_async_copy(a, b, lsem.at[i])
        for i, (a, b) in enumerate(((q_hbm, q), (ku_hbm, ku), (vu_hbm, vu), (w_hbm, w)))
    ]
    for load in loads:
        load.start()

    barrier = pltpu.get_barrier_semaphore()
    has_left, has_right = me > 0, me < n - 1

    def greet(**where):
        pl.semaphore_signal(
            barrier, inc=1, device_id=where, device_id_type=pl.DeviceIdType.MESH
        )

    @pl.when(has_left)
    def _():
        greet(seq=me - 1)

    @pl.when(has_right)
    def _():
        greet(seq=me + 1)

    for s in range(1, xn):
        greet(head=lax.rem(xi + s, xn))

    kr = tokens // xn
    twice = jnp.concatenate([rope_ref[...], rope_ref[...]], axis=1)
    for part in range(xn):
        rows = slice(part * kr, (part + 1) * kr)
        keys[me * xn + part, :, :lat] = lat_ref[rows, :]
        keys[me * xn + part, :, lat:] = twice[rows]

    met = xn - 1 + jnp.minimum(me, 1) + jnp.minimum(n - 1 - me, 1)
    pl.semaphore_wait(barrier, met)

    def kv_copy(i, way):
        return pltpu.make_async_remote_copy(
            src_ref=keys.at[i],
            dst_ref=keys.at[i],
            send_sem=kv_ssem.at[way, i],
            recv_sem=kv_rsem.at[i],
            device_id={"seq": me - 1 + 2 * way},
            device_id_type=pl.DeviceIdType.MESH,
        )

    def kx_copy(i, s):
        return pltpu.make_async_remote_copy(
            src_ref=keys.at[i],
            dst_ref=keys.at[i],
            send_sem=kx_ssem.at[s, i],
            recv_sem=kv_rsem.at[i],
            device_id={"head": lax.rem(xi + s, xn)},
            device_id_type=pl.DeviceIdType.MESH,
        )

    def z_copy(unit, hg, way):
        return pltpu.make_async_remote_copy(
            src_ref=full.at[unit, hg],
            dst_ref=full.at[unit, hg],
            send_sem=z_ssem.at[way, unit, hg],
            recv_sem=z_rsem.at[unit, hg],
            device_id={"seq": me - 1 + 2 * way},
            device_id_type=pl.DeviceIdType.MESH,
        )

    def send_own(make):
        @pl.when(has_left)
        def _():
            make(0).start()

        @pl.when(has_right)
        def _():
            make(1).start()

    def take(make, d, after=None):
        @pl.when(me + d < n)
        def _():
            make(me + d, 1).wait_recv()

            @pl.when(has_left)
            def _():
                make(me + d, 0).start()

            if after is not None:
                after(me + d)

        @pl.when(me - d >= 0)
        def _():
            make(me - d, 0).wait_recv()

            @pl.when(has_right)
            def _():
                make(me - d, 1).start()

            if after is not None:
                after(me - d)

    send_own(lambda way: kv_copy(me * xn + xi, way))

    def share(src):
        for s in range(1, xn):
            kx_copy(src * xn + xi, s).start()

    def absorb(i, _):
        block = q[:, pl.ds(pl.multiple_of(i * pair, pair), pair)]
        lead = jnp.zeros((rope, lat), bf16)
        tail = lead
        first = jnp.dot(block[:, :nope], ku[2 * i], preferred_element_type=f32)
        second = jnp.dot(
            block[:, nope:],
            jnp.concatenate([lead, ku[2 * i + 1], tail], axis=0),
            preferred_element_type=f32,
        )
        lane = lax.broadcasted_iota(jnp.int32, (tokens, 2 * rope), 1)
        zero = jnp.zeros((tokens, 2 * rope), bf16)
        wide[2 * i, :, :lat] = first.astype(bf16)
        wide[2 * i + 1, :, :lat] = second.astype(bf16)
        wide[2 * i, :, lat:] = jnp.where(lane < rope, block[:, nope : nope + 2 * rope], zero)
        wide[2 * i + 1, :, lat:] = jnp.where(lane >= rope, block[:, pair - 2 * rope :], zero)
        return 0

    loads[0].wait()
    loads[1].wait()

    span_len = ctx // NSPAN
    span = me * tokens // span_len
    first_pos = start_ref[0, span]
    prefix = prefix_ref[0, span]
    row_pos = first_pos + me * tokens % span_len + lax.broadcasted_iota(jnp.int32, (tokens, ctx), 0)
    key_pos = lax.broadcasted_iota(jnp.int32, (tokens, ctx), 1)
    visible = (key_pos < prefix) | ((key_pos >= first_pos) & (key_pos <= row_pos))
    bias[...] = jnp.where(visible, 0.0, masked_fill)

    half = heads // 4
    lax.fori_loop(0, half, absorb, 0)
    for d in range(1, n):
        take(lambda src, way: kv_copy(src * xn + xi, way), d, share)
        if d == 1:
            lax.fori_loop(half, heads // 2, absorb, 0)

    def shared(src, _):
        @pl.when(src != me)
        def _():
            for s in range(1, xn):
                kx_copy(src * xn + lax.rem(xi + s, xn), s).wait_recv()

        return 0

    lax.fori_loop(0, n, shared, 0)
    loads[2].wait()

    def attend(m, _):
        tb, hg = m // hgs, lax.rem(m, hgs)
        rows = pl.ds(pl.multiple_of(tb * ts, ts), ts)
        unit = me * SPLIT + tb
        all_keys = keys[...].reshape(ctx, keys.shape[2])
        hide = jnp.concatenate([bias[rows, :]] * batch, axis=0)
        for p in range(hg_heads // batch):
            h = hg * hg_heads + batch * p
            wq = wide[pl.ds(h, batch), rows, :].reshape(batch * ts, wide.shape[2])
            scores = lax.dot_general(
                wq, all_keys, (((1,), (1,)), ((), ())), preferred_element_type=f32
            )
            scores = scores * scale + hide
            peak = jnp.max(scores, axis=1, keepdims=True)
            weights = jnp.exp2(scores - peak)
            total = jnp.sum(weights, axis=1, keepdims=True)
            mixed = jnp.dot(weights.astype(bf16), all_keys[:, :lat], preferred_element_type=f32)
            mixed = (mixed / total).astype(bf16)
            for k in range(batch):
                value = jnp.dot(
                    mixed[k * ts : (k + 1) * ts], vu[h + k], preferred_element_type=f32
                )
                lo = (batch * p + k) * vdim
                full[unit, hg, :, lo : lo + vdim] = value.astype(bf16)
        send_own(lambda way: z_copy(unit, hg, way))
        return 0

    lax.fori_loop(0, SPLIT * hgs, attend, 0)

    def x_copy(unit, t):
        return pltpu.make_async_remote_copy(
            src_ref=xs.at[unit, t],
            dst_ref=xr.at[xi, lax.rem(unit, upx), t],
            send_sem=x_ssem.at[unit, t],
            recv_sem=x_rsem.at[xi, lax.rem(unit, upx), t],
            device_id={"head": unit // upx},
            device_id_type=pl.DeviceIdType.MESH,
        )

    def project(unit):
        mine = unit // upx == xi

        def tile(t, _):
            total = jnp.zeros((ts, nt), f32)
            for hg in range(hgs):
                if ntiles == 1:
                    part = w[hg * hw : (hg + 1) * hw, :]
                else:
                    part = w[hg * hw : (hg + 1) * hw, pl.ds(pl.multiple_of(t * nt, nt), nt)]
                total += jnp.dot(full[unit, hg], part, preferred_element_type=f32)

            @pl.when(mine)
            def _():
                acc[lax.rem(unit, upx), t] = total

            @pl.when(jnp.logical_not(mine))
            def _():
                xs[unit, t] = total.astype(bf16)
                x_copy(unit, t).start()

            return 0

        lax.fori_loop(0, ntiles, tile, 0)

    loads[3].wait()

    for tb in range(SPLIT):
        project(me * SPLIT + tb)

    def gather(i, _):
        d, tb = 1 + i // SPLIT, lax.rem(i, SPLIT)
        for hg in range(hgs):
            take(lambda src, way, hg=hg: z_copy(src * SPLIT + tb, hg, way), d)

        @pl.when(me + d < n)
        def _():
            project((me + d) * SPLIT + tb)

        @pl.when(me - d >= 0)
        def _():
            project((me - d) * SPLIT + tb)

        return 0

    lax.fori_loop(0, (n - 1) * SPLIT, gather, 0)

    def sent(i, _):
        unit = i
        left = has_left & (unit >= me * SPLIT)
        right = has_right & (unit < (me + 1) * SPLIT)
        for way, did in ((0, left), (1, right)):

            @pl.when(did)
            def _():
                for hg in range(hgs):
                    z_copy(unit, hg, way).wait_send()

        return 0

    lax.fori_loop(0, units, sent, 0)

    def kv_sent(src, _):
        @pl.when(has_left & (src >= me))
        def _():
            kv_copy(src * xn + xi, 0).wait_send()

        @pl.when(has_right & (src <= me))
        def _():
            kv_copy(src * xn + xi, 1).wait_send()

        @pl.when(src != me)
        def _():
            for s in range(1, xn):
                kx_copy(src * xn + xi, s).wait_send()

        return 0

    lax.fori_loop(0, n, kv_sent, 0)

    for lu in range(upx):
        for t in range(ntiles):
            total = acc[lu, t]
            for s in range(1, xn):
                peer = lax.rem(xi + s, xn)
                pltpu.make_async_remote_copy(
                    src_ref=xs.at[0, t],
                    dst_ref=xr.at[peer, lu, t],
                    send_sem=x_ssem.at[0, t],
                    recv_sem=x_rsem.at[peer, lu, t],
                    device_id={"head": peer},
                    device_id_type=pl.DeviceIdType.MESH,
                ).wait_recv()
                total = total + xr[peer, lu, t].astype(f32)
            out_ref[lu * ts : (lu + 1) * ts, t * nt : (t + 1) * nt] = total.astype(bf16)

    def x_sent(i, _):
        @pl.when(i // upx != xi)
        def _():
            for t in range(ntiles):
                x_copy(i, t).wait_send()

        return 0

    lax.fori_loop(0, units, x_sent, 0)


def on_device(
    n, xn, q_heads, cache_latent, cache_rope, span_start, prefix_len, key_up, value_up, out_weight
):
    heads, nope, lat = key_up.shape[1:]
    vdim = value_up.shape[3]
    tokens = q_heads.shape[1]
    rope = cache_rope.shape[2]
    rows_all, width = out_weight.shape[1:]
    kw = lat + 2 * rope
    ts = tokens // SPLIT
    units = n * SPLIT
    upx = units // xn
    hg_heads = math.gcd(16, heads)
    hgs = heads // hg_heads
    nt = 256 if width % 256 == 0 else width
    ntiles = width // nt
    ctx = n * tokens
    vmem, smem = pltpu.VMEM, pltpu.SMEM
    hbm = pl.BlockSpec(memory_space=pl.ANY)
    out = pl.pallas_call(
        functools.partial(kernel, n, xn),
        out_shape=jax.ShapeDtypeStruct((upx * ts, width), bf16),
        in_specs=[
            pl.BlockSpec(memory_space=vmem),
            pl.BlockSpec(memory_space=vmem),
            pl.BlockSpec(memory_space=smem),
            pl.BlockSpec(memory_space=smem),
            hbm,
            hbm,
            hbm,
            hbm,
        ],
        out_specs=pl.BlockSpec(memory_space=vmem),
        scratch_shapes=[
            vmem((n * xn, tokens // xn, kw), bf16),
            vmem(q_heads.shape[1:], bf16),
            vmem(key_up.shape[1:], bf16),
            vmem(value_up.shape[1:], bf16),
            vmem((rows_all, width), bf16),
            vmem((heads, tokens, kw), bf16),
            vmem((tokens, ctx), f32),
            vmem((units, hgs, ts, hg_heads * vdim), bf16),
            vmem((upx, ntiles, ts, nt), f32),
            vmem((units, ntiles, ts, nt), bf16),
            vmem((xn, upx, ntiles, ts, nt), bf16),
            pltpu.SemaphoreType.DMA((4,)),
            pltpu.SemaphoreType.DMA((2, n * xn)),
            pltpu.SemaphoreType.DMA((n * xn,)),
            pltpu.SemaphoreType.DMA((xn, n * xn)),
            pltpu.SemaphoreType.DMA((2, units, hgs)),
            pltpu.SemaphoreType.DMA((units, hgs)),
            pltpu.SemaphoreType.DMA((units, ntiles)),
            pltpu.SemaphoreType.DMA((xn, upx, ntiles)),
        ],
        compiler_params=pltpu.CompilerParams(
            collective_id=0, has_side_effects=True, vmem_limit_bytes=56 * 1024 * 1024
        ),
        cost_estimate=pl.CostEstimate(
            flops=2 * ctx * rows_all * width + 4 * tokens * heads * ctx * kw,
            bytes_accessed=2 * rows_all * width,
            transcendentals=tokens * heads * ctx,
        ),
    )(cache_latent[0], cache_rope[0], span_start, prefix_len, q_heads[0], key_up[0], value_up[0], out_weight[0])
    return out[None]


def solution(mesh):
    in_specs = (
        P("section", ("groups", "seq"), "head"),
        P("section", ("groups", "seq"), None),
        P("section", ("groups", "seq"), None),
        P("section", "groups"),
        P("section", "groups"),
        P("section", "head", None, None),
        P("section", "head", None, None),
        P("section", "head", "seq"),
    )
    out_specs = P("section", ("groups", "head"), "seq")
    return jax.shard_map(
        functools.partial(on_device, mesh.shape["seq"], mesh.shape["head"]),
        mesh=mesh,
        in_specs=in_specs,
        out_specs=out_specs,
        check_vma=False,
    )
```

```python
import functools
import math

import jax
import jax.numpy as jnp
from jax import lax
from jax.experimental import pallas as pl
from jax.experimental.pallas import tpu as pltpu
from jax.sharding import PartitionSpec as P

NSPAN = 2
SPLIT = 2
masked_fill = -1e30
f32, bf16 = jnp.float32, jnp.bfloat16


def kernel(
    n, xn, lat_ref, rope_ref, start_ref, prefix_ref, q_hbm, ku_hbm, vu_hbm, w_hbm, out_ref,
    keys, q, ku, vu, w, wide, bias, full, acc, xs, xr,
    lsem, kv_ssem, kv_rsem, kx_ssem, z_ssem, z_rsem, x_ssem, x_rsem,
):
    me = lax.axis_index("seq")
    xi = lax.axis_index("head")
    tokens = lat_ref.shape[0]
    heads, nope, lat = ku.shape
    vdim = vu.shape[2]
    pair = 2 * q.shape[1] // heads
    rope = pair // 2 - nope
    units, hgs, ts, hw = full.shape
    hg_heads = hw // vdim
    batch = 2
    upx, ntiles, _, nt = acc.shape
    ctx = n * tokens
    scale = math.log2(math.e) * (pair // 2) ** (-0.5)

    loads = [
        pltpu.make_async_copy(a, b, lsem.at[i])
        for i, (a, b) in enumerate(((q_hbm, q), (ku_hbm, ku), (vu_hbm, vu), (w_hbm, w)))
    ]
    for load in loads:
        load.start()

    barrier = pltpu.get_barrier_semaphore()
    has_left, has_right = me > 0, me < n - 1

    def greet(**where):
        pl.semaphore_signal(
            barrier, inc=1, device_id=where, device_id_type=pl.DeviceIdType.MESH
        )

    @pl.when(has_left)
    def _():
        greet(seq=me - 1)

    @pl.when(has_right)
    def _():
        greet(seq=me + 1)

    for s in range(1, xn):
        greet(head=lax.rem(xi + s, xn))

    kr = tokens // xn
    twice = jnp.concatenate([rope_ref[...], rope_ref[...]], axis=1)
    for part in range(xn):
        rows = slice(part * kr, (part + 1) * kr)
        keys[me * xn + part, :, :lat] = lat_ref[rows, :]
        keys[me * xn + part, :, lat:] = twice[rows]

    met = xn - 1 + jnp.minimum(me, 1) + jnp.minimum(n - 1 - me, 1)
    pl.semaphore_wait(barrier, met)

    def kv_copy(i, way):
        return pltpu.make_async_remote_copy(
            src_ref=keys.at[i],
            dst_ref=keys.at[i],
            send_sem=kv_ssem.at[way, i],
            recv_sem=kv_rsem.at[i],
            device_id={"seq": me - 1 + 2 * way},
            device_id_type=pl.DeviceIdType.MESH,
        )

    def kx_copy(i, s):
        return pltpu.make_async_remote_copy(
            src_ref=keys.at[i],
            dst_ref=keys.at[i],
            send_sem=kx_ssem.at[s, i],
            recv_sem=kv_rsem.at[i],
            device_id={"head": lax.rem(xi + s, xn)},
            device_id_type=pl.DeviceIdType.MESH,
        )

    def z_copy(unit, hg, way):
        return pltpu.make_async_remote_copy(
            src_ref=full.at[unit, hg],
            dst_ref=full.at[unit, hg],
            send_sem=z_ssem.at[way, unit, hg],
            recv_sem=z_rsem.at[unit, hg],
            device_id={"seq": me - 1 + 2 * way},
            device_id_type=pl.DeviceIdType.MESH,
        )

    def send_own(make):
        @pl.when(has_left)
        def _():
            make(0).start()

        @pl.when(has_right)
        def _():
            make(1).start()

    def take(make, d, after=None):
        @pl.when(me + d < n)
        def _():
            make(me + d, 1).wait_recv()

            @pl.when(has_left)
            def _():
                make(me + d, 0).start()

            if after is not None:
                after(me + d)

        @pl.when(me - d >= 0)
        def _():
            make(me - d, 0).wait_recv()

            @pl.when(has_right)
            def _():
                make(me - d, 1).start()

            if after is not None:
                after(me - d)

    send_own(lambda way: kv_copy(me * xn + xi, way))

    def share(src):
        for s in range(1, xn):
            kx_copy(src * xn + xi, s).start()

    def absorb(i, _):
        block = q[:, pl.ds(pl.multiple_of(i * pair, pair), pair)]
        lead = jnp.zeros((rope, lat), bf16)
        tail = lead
        first = jnp.dot(block[:, :nope], ku[2 * i], preferred_element_type=f32)
        second = jnp.dot(
            block[:, nope:],
            jnp.concatenate([lead, ku[2 * i + 1], tail], axis=0),
            preferred_element_type=f32,
        )
        lane = lax.broadcasted_iota(jnp.int32, (tokens, 2 * rope), 1)
        zero = jnp.zeros((tokens, 2 * rope), bf16)
        wide[2 * i, :, :lat] = first.astype(bf16)
        wide[2 * i + 1, :, :lat] = second.astype(bf16)
        wide[2 * i, :, lat:] = jnp.where(lane < rope, block[:, nope : nope + 2 * rope], zero)
        wide[2 * i + 1, :, lat:] = jnp.where(lane >= rope, block[:, pair - 2 * rope :], zero)
        return 0

    loads[0].wait()
    loads[1].wait()

    span_len = ctx // NSPAN
    span = me * tokens // span_len
    first_pos = start_ref[0, span]
    prefix = prefix_ref[0, span]
    row_pos = first_pos + me * tokens % span_len + lax.broadcasted_iota(jnp.int32, (tokens, ctx), 0)
    key_pos = lax.broadcasted_iota(jnp.int32, (tokens, ctx), 1)
    visible = (key_pos < prefix) | ((key_pos >= first_pos) & (key_pos <= row_pos))
    bias[...] = jnp.where(visible, 0.0, masked_fill)

    half = heads // 4
    lax.fori_loop(0, half, absorb, 0)
    for d in range(1, n):
        take(lambda src, way: kv_copy(src * xn + xi, way), d, share)
        if d == 1:
            lax.fori_loop(half, heads // 2, absorb, 0)

    def shared(src, _):
        @pl.when(src != me)
        def _():
            for s in range(1, xn):
                kx_copy(src * xn + lax.rem(xi + s, xn), s).wait_recv()

        return 0

    lax.fori_loop(0, n, shared, 0)
    loads[2].wait()

    def attend(m, _):
        tb, hg = m // hgs, lax.rem(m, hgs)
        rows = pl.ds(pl.multiple_of(tb * ts, ts), ts)
        unit = me * SPLIT + tb
        all_keys = keys[...].reshape(ctx, keys.shape[2])
        hide = jnp.concatenate([bias[rows, :]] * batch, axis=0)
        for p in range(hg_heads // batch):
            h = hg * hg_heads + batch * p
            wq = wide[pl.ds(h, batch), rows, :].reshape(batch * ts, wide.shape[2])
            scores = lax.dot_general(
                wq, all_keys, (((1,), (1,)), ((), ())), preferred_element_type=f32
            )
            scores = scores * scale + hide
            peak = jnp.max(scores, axis=1, keepdims=True)
            weights = jnp.exp2(scores - peak)
            total = jnp.sum(weights, axis=1, keepdims=True)
            mixed = jnp.dot(weights.astype(bf16), all_keys[:, :lat], preferred_element_type=f32)
            mixed = (mixed / total).astype(bf16)
            for k in range(batch):
                value = jnp.dot(
                    mixed[k * ts : (k + 1) * ts], vu[h + k], preferred_element_type=f32
                )
                lo = (batch * p + k) * vdim
                full[unit, hg, :, lo : lo + vdim] = value.astype(bf16)
        send_own(lambda way: z_copy(unit, hg, way))
        return 0

    lax.fori_loop(0, SPLIT * hgs, attend, 0)

    def x_copy(unit, t):
        return pltpu.make_async_remote_copy(
            src_ref=xs.at[unit, t],
            dst_ref=xr.at[xi, lax.rem(unit, upx), t],
            send_sem=x_ssem.at[unit, t],
            recv_sem=x_rsem.at[xi, lax.rem(unit, upx), t],
            device_id={"head": unit // upx},
            device_id_type=pl.DeviceIdType.MESH,
        )

    def project(unit):
        mine = unit // upx == xi

        def tile(t, _):
            total = jnp.zeros((ts, nt), f32)
            for hg in range(hgs):
                if ntiles == 1:
                    part = w[hg * hw : (hg + 1) * hw, :]
                else:
                    part = w[hg * hw : (hg + 1) * hw, pl.ds(pl.multiple_of(t * nt, nt), nt)]
                total += jnp.dot(full[unit, hg], part, preferred_element_type=f32)

            @pl.when(mine)
            def _():
                acc[lax.rem(unit, upx), t] = total

            @pl.when(jnp.logical_not(mine))
            def _():
                xs[unit, t] = total.astype(bf16)
                x_copy(unit, t).start()

            return 0

        lax.fori_loop(0, ntiles, tile, 0)

    loads[3].wait()

    for tb in range(SPLIT):
        project(me * SPLIT + tb)

    def gather(i, _):
        d, tb = 1 + i // SPLIT, lax.rem(i, SPLIT)
        for hg in range(hgs):
            take(lambda src, way, hg=hg: z_copy(src * SPLIT + tb, hg, way), d)

        @pl.when(me + d < n)
        def _():
            project((me + d) * SPLIT + tb)

        @pl.when(me - d >= 0)
        def _():
            project((me - d) * SPLIT + tb)

        return 0

    lax.fori_loop(0, (n - 1) * SPLIT, gather, 0)

    def sent(i, _):
        unit = i
        left = has_left & (unit >= me * SPLIT)
        right = has_right & (unit < (me + 1) * SPLIT)
        for way, did in ((0, left), (1, right)):

            @pl.when(did)
            def _():
                for hg in range(hgs):
                    z_copy(unit, hg, way).wait_send()

        return 0

    lax.fori_loop(0, units, sent, 0)

    def kv_sent(src, _):
        @pl.when(has_left & (src >= me))
        def _():
            kv_copy(src * xn + xi, 0).wait_send()

        @pl.when(has_right & (src <= me))
        def _():
            kv_copy(src * xn + xi, 1).wait_send()

        @pl.when(src != me)
        def _():
            for s in range(1, xn):
                kx_copy(src * xn + xi, s).wait_send()

        return 0

    lax.fori_loop(0, n, kv_sent, 0)

    for lu in range(upx):
        for t in range(ntiles):
            total = acc[lu, t]
            for s in range(1, xn):
                peer = lax.rem(xi + s, xn)
                pltpu.make_async_remote_copy(
                    src_ref=xs.at[0, t],
                    dst_ref=xr.at[peer, lu, t],
                    send_sem=x_ssem.at[0, t],
                    recv_sem=x_rsem.at[peer, lu, t],
                    device_id={"head": peer},
                    device_id_type=pl.DeviceIdType.MESH,
                ).wait_recv()
                total = total + xr[peer, lu, t].astype(f32)
            out_ref[lu * ts : (lu + 1) * ts, t * nt : (t + 1) * nt] = total.astype(bf16)

    def x_sent(i, _):
        @pl.when(i // upx != xi)
        def _():
            for t in range(ntiles):
                x_copy(i, t).wait_send()

        return 0

    lax.fori_loop(0, units, x_sent, 0)


def on_device(
    n, xn, q_heads, cache_latent, cache_rope, span_start, prefix_len, key_up, value_up, out_weight
):
    heads, nope, lat = key_up.shape[1:]
    vdim = value_up.shape[3]
    tokens = q_heads.shape[1]
    rope = cache_rope.shape[2]
    rows_all, width = out_weight.shape[1:]
    kw = lat + 2 * rope
    ts = tokens // SPLIT
    units = n * SPLIT
    upx = units // xn
    hg_heads = math.gcd(8, heads)
    hgs = heads // hg_heads
    nt = 256 if width % 256 == 0 else width
    ntiles = width // nt
    ctx = n * tokens
    vmem, smem = pltpu.VMEM, pltpu.SMEM
    hbm = pl.BlockSpec(memory_space=pl.ANY)
    out = pl.pallas_call(
        functools.partial(kernel, n, xn),
        out_shape=jax.ShapeDtypeStruct((upx * ts, width), bf16),
        in_specs=[
            pl.BlockSpec(memory_space=vmem),
            pl.BlockSpec(memory_space=vmem),
            pl.BlockSpec(memory_space=smem),
            pl.BlockSpec(memory_space=smem),
            hbm,
            hbm,
            hbm,
            hbm,
        ],
        out_specs=pl.BlockSpec(memory_space=vmem),
        scratch_shapes=[
            vmem((n * xn, tokens // xn, kw), bf16),
            vmem(q_heads.shape[1:], bf16),
            vmem(key_up.shape[1:], bf16),
            vmem(value_up.shape[1:], bf16),
            vmem((rows_all, width), bf16),
            vmem((heads, tokens, kw), bf16),
            vmem((tokens, ctx), f32),
            vmem((units, hgs, ts, hg_heads * vdim), bf16),
            vmem((upx, ntiles, ts, nt), f32),
            vmem((units, ntiles, ts, nt), bf16),
            vmem((xn, upx, ntiles, ts, nt), bf16),
            pltpu.SemaphoreType.DMA((4,)),
            pltpu.SemaphoreType.DMA((2, n * xn)),
            pltpu.SemaphoreType.DMA((n * xn,)),
            pltpu.SemaphoreType.DMA((xn, n * xn)),
            pltpu.SemaphoreType.DMA((2, units, hgs)),
            pltpu.SemaphoreType.DMA((units, hgs)),
            pltpu.SemaphoreType.DMA((units, ntiles)),
            pltpu.SemaphoreType.DMA((xn, upx, ntiles)),
        ],
        compiler_params=pltpu.CompilerParams(
            collective_id=0, has_side_effects=True, vmem_limit_bytes=56 * 1024 * 1024
        ),
        cost_estimate=pl.CostEstimate(
            flops=2 * ctx * rows_all * width + 4 * tokens * heads * ctx * kw,
            bytes_accessed=2 * rows_all * width,
            transcendentals=tokens * heads * ctx,
        ),
    )(cache_latent[0], cache_rope[0], span_start, prefix_len, q_heads[0], key_up[0], value_up[0], out_weight[0])
    return out[None]


def solution(mesh):
    in_specs = (
        P("section", ("groups", "seq"), "head"),
        P("section", ("groups", "seq"), None),
        P("section", ("groups", "seq"), None),
        P("section", "groups"),
        P("section", "groups"),
        P("section", "head", None, None),
        P("section", "head", None, None),
        P("section", "head", "seq"),
    )
    out_specs = P("section", ("groups", "head"), "seq")
    return jax.shard_map(
        functools.partial(on_device, mesh.shape["seq"], mesh.shape["head"]),
        mesh=mesh,
        in_specs=in_specs,
        out_specs=out_specs,
        check_vma=False,
    )
```
